512 devices in a mesh: rep: 32 (over y, x, core), tp: 16 (over z).
Axes of the slice: x: 4, y: 4, z: 16, core: 2. Of those that a mesh axis runs over, the one named last changes fastest.
Arguments:
- queries: bfloat16 [1024, 4096], P('rep', 'tp'), may hold values from -110 to 110
- new_key_value: bfloat16 [1024, 16, 256], P('rep', 'tp'), may hold values from -6 to 6
- key_value_cache: bfloat16 [1024, 16, 128, 256], P('rep', 'tp'), may hold values from -4 to 4
- lengths: int32 [1024], P('rep'), may hold values from 2 to 128
- residual: bfloat16 [1024, 4096], P('rep', 'tp'), may hold values from -1.1953125 to 1.1953125
- output_weight: bfloat16 [4096, 4096], P('tp'), may hold values from -0.09375 to 0.09375
- row_adapter_index: int32 [1024], P('rep'), may hold values from 0 to 127, as said below
- adapter_storage_slot: int32 [128], replicated, may hold values from 0 to 127, as said below
- adapter_down_weight: bfloat16 [128, 4096, 64], P('rep', 'tp'), may hold values from -0.09375 to 0.09375
- adapter_up_weight: bfloat16 [128, 64, 4096], P('rep', None, 'tp'), may hold values from -0.75 to 0.75
Outputs:
- layer_out: bfloat16 [1024, 4096], P('rep', 'tp')
The draws below stay inside these ranges and needn't reach their ends.
Inputs may be any that keep to these rules, and one draw needn't show every extreme that they name: adapter_storage_slot holds each of 0 to 127 once. `row_adapter_index`: within the 32 rows of one index of rep, at most 4 rows use adapters with the same adapter_storage_slot // 4, and in every such block some value of it is used by exactly 4 rows.
All inputs are finite; a program needn't handle non-finite values.
Results may differ from the reference program's by a relative error of at most 0.0085.
Values may be sent and summed in bfloat16 or wider, within the bound.
No kernel may reach another device: no remote copies, remote signals or barrier semaphores. Data moves between devices by JAX's collectives and lax.ppermute only.
A program may use at most 64 MiB of HBM per device.

```python
import math
import jax
import jax.numpy as jnp
from jax import lax

ROWS_PER_SHARD = 32
CTX = 128
ADAPT_DEV = 4
QUERY_HEADS = 32
HEAD_WIDTH = 128
OUTPUT_FEATURES = 4096
ADAPTER_RANK = 64
DECODE_ROWS = 1024
ADAPTER_TOTAL = 128
CAP = 4
N_REP = 32
N_TP = 16


def shared_slots(key):
    return jax.random.permutation(jax.random.fold_in(key, 7), ADAPTER_TOTAL).astype(jnp.int32)


def shared_cache(key):
    return jax.random.truncated_normal(jax.random.fold_in(key, 21), -4.0, 4.0, (DECODE_ROWS, N_TP, CTX, 2 * HEAD_WIDTH), jnp.float32)


def draw_adapter_storage_slot(key, part):
    return shared_slots(key)


def draw_row_adapter_index(key, part):
    slot_table = shared_slots(key)
    inverse = jnp.argsort(slot_table, stable=True).astype(jnp.int32)
    slot_total = N_REP * CAP
    owner_weight = jnp.left_shift(jnp.int32(1), jax.random.randint(jax.random.fold_in(key, 11), (N_REP,), 0, 7).astype(jnp.int32))
    position = jnp.arange(slot_total, dtype=jnp.int32)
    owner_of = position // CAP

    def one_block(device):
        sub_key = jax.random.fold_in(key, 1000 + device)
        key_one, key_two, key_three, key_four = jax.random.split(sub_key, 4)
        hot_owner = jax.random.randint(key_one, (), 0, N_REP).astype(jnp.int32)
        base_score = jax.random.randint(key_two, (slot_total,), 0, 1024).astype(jnp.int32) * owner_weight[owner_of]
        scores = base_score * slot_total + position + jnp.where(owner_of == hot_owner, jnp.int32(1 << 29), jnp.int32(0))
        chosen = lax.top_k(scores, ROWS_PER_SHARD)[1].astype(jnp.int32)
        owner_row = chosen // CAP
        local_idx = jnp.minimum(jax.random.randint(key_three, (ROWS_PER_SHARD,), 0, ADAPT_DEV), jax.random.randint(key_four, (ROWS_PER_SHARD,), 0, ADAPT_DEV)).astype(jnp.int32)
        return inverse[owner_row * ADAPT_DEV + local_idx]
    return jax.vmap(one_block)(jnp.arange(N_REP, dtype=jnp.int32)).reshape(DECODE_ROWS).astype(jnp.int32)


def draw_key_value_cache(key, part):
    cache_all = shared_cache(key)
    return cache_all.astype(jnp.bfloat16)


def draw_queries(key, part):
    normal_rows = jax.random.truncated_normal(jax.random.fold_in(key, 22), -4.0, 4.0, (DECODE_ROWS, QUERY_HEADS, HEAD_WIDTH), jnp.float32)
    return normal_rows.reshape(DECODE_ROWS, QUERY_HEADS * HEAD_WIDTH).astype(jnp.bfloat16)


def plant(values, own_key, least, largest):
    dims = values.shape
    index_at = [jax.random.randint(jax.random.fold_in(own_key, axis), (), 0, dims[axis]) for axis in range(len(dims))]
    values = values.at[tuple(index_at)].set(least)
    longest = dims.index(max(dims))
    index_at[longest] = (index_at[longest] + 1) % dims[longest]
    return values.at[tuple(index_at)].set(largest)


def block_levels(rng, shape, cuts, smallest, high):
    def one(axis_at, shards_of):
        heights = jax.random.uniform(jax.random.fold_in(jax.random.fold_in(rng, 6), axis_at), (shards_of,), jnp.float32, smallest / len(cuts), high / len(cuts))
        return jnp.repeat(jnp.exp(heights), shape[axis_at] // shards_of).reshape((-1,) + (1,) * (len(shape) - axis_at - 1))

    loudness = one(*cuts[0])
    for cut in cuts[1:]:
        loudness = loudness * one(*cut)
    return loudness


def centred(stream_key, dims, scale, limit, shards=(), held_as=jnp.bfloat16):
    drawn = jax.random.normal(stream_key, dims, jnp.float32) * scale
    if len(shards) > 0:
        drawn = block_levels(stream_key, dims, shards, -0.22, 0.18) * drawn
    return jnp.clip(drawn, min=-limit, max=limit).astype(held_as)


def setup_inputs(seed: int = 0) -> dict:
    seeds = jax.random.split(jax.random.key(seed), 11)
    return {
        "queries": draw_queries(jax.random.fold_in(seeds[10], 71), 0),
        "new_key_value": centred(seeds[1], (DECODE_ROWS, N_TP, 2 * HEAD_WIDTH), 1.0, 6.0, ((0, 32), (1, 16))),
        "key_value_cache": draw_key_value_cache(jax.random.fold_in(seeds[10], 71), 0),
        "lengths": plant(jax.random.randint(seeds[3], (DECODE_ROWS,), 2, CTX + 1), jax.random.fold_in(seeds[3], 1), 2, CTX).astype(jnp.int32),
        "residual": centred(seeds[4], (DECODE_ROWS, OUTPUT_FEATURES), 0.2, 1.1953125, ((0, 32), (1, 16))),
        "output_weight": centred(seeds[5], (QUERY_HEADS * HEAD_WIDTH, OUTPUT_FEATURES), (QUERY_HEADS * HEAD_WIDTH) ** -0.5, 0.09375, ((0, 16),)),
        "row_adapter_index": draw_row_adapter_index(jax.random.fold_in(seeds[10], 71), 0),
        "adapter_storage_slot": draw_adapter_storage_slot(jax.random.fold_in(seeds[10], 71), 0),
        "adapter_down_weight": centred(seeds[8], (ADAPTER_TOTAL, QUERY_HEADS * HEAD_WIDTH, ADAPTER_RANK), (QUERY_HEADS * HEAD_WIDTH) ** -0.5, 0.09375, ((0, 32), (1, 16))),
        "adapter_up_weight": centred(seeds[9], (ADAPTER_TOTAL, ADAPTER_RANK, OUTPUT_FEATURES), ADAPTER_RANK ** -0.5, 0.75, ((0, 32), (2, 16))),
    }


def attention_block(queries, kv_block, fresh_kv, length):
    row_count = queries.shape[0]
    per_slot = QUERY_HEADS // N_TP
    heads = queries.astype(jnp.float32).reshape(row_count, N_TP, per_slot, HEAD_WIDTH)
    key_rows = kv_block[..., :HEAD_WIDTH].astype(jnp.float32)
    value_rows = kv_block[..., HEAD_WIDTH:].astype(jnp.float32)
    score_scale = 1.0 / math.sqrt(HEAD_WIDTH)
    scores = jnp.einsum('btqd,btcd->btqc', heads, key_rows) * score_scale
    own_score = jnp.einsum('btqd,btd->btq', heads, fresh_kv[..., :HEAD_WIDTH].astype(jnp.float32)) * score_scale
    live_mask = (jnp.arange(CTX, dtype=jnp.int32)[None, :] < length[:, None])[:, None, None, :]
    scores = jnp.where(live_mask, scores, -1e+30)
    row_max = jnp.maximum(lax.optimization_barrier(jnp.max(scores, axis=-1)), own_score)
    weights = jnp.where(live_mask, jnp.exp(scores - row_max[..., None]), 0.0)
    own_weight = jnp.exp(own_score - row_max)
    denom = lax.optimization_barrier(jnp.sum(weights, axis=-1)) + own_weight
    weights_bf = (weights / denom[..., None]).astype(jnp.bfloat16)
    own_bf = (own_weight / denom).astype(jnp.bfloat16)
    mixed_out = jnp.einsum('btqc,btcd->btqd', weights_bf.astype(jnp.float32), value_rows)
    mixed_out = mixed_out + own_bf.astype(jnp.float32)[..., None] * fresh_kv[..., HEAD_WIDTH:].astype(jnp.float32)[:, :, None, :]
    return mixed_out.reshape(row_count, QUERY_HEADS * HEAD_WIDTH).astype(jnp.bfloat16)

def reference(queries, new_key_value, key_value_cache, lengths, residual, output_weight, row_adapter_index, adapter_storage_slot, adapter_down_weight, adapter_up_weight):
    block_list = DECODE_ROWS // ROWS_PER_SHARD

    def attend_one(inputs):
        return attention_block(inputs[0], inputs[1], inputs[2], inputs[3])
    attention_result = lax.map(attend_one, (queries.reshape(block_list, ROWS_PER_SHARD, QUERY_HEADS * HEAD_WIDTH), key_value_cache.reshape(block_list, ROWS_PER_SHARD, N_TP, CTX, 2 * HEAD_WIDTH), new_key_value.reshape(block_list, ROWS_PER_SHARD, N_TP, 2 * HEAD_WIDTH), lengths.reshape(block_list, ROWS_PER_SHARD))).reshape(DECODE_ROWS, QUERY_HEADS * HEAD_WIDTH)
    plain_output = jnp.dot(attention_result, output_weight, preferred_element_type=jnp.float32)
    row_storage_slot = adapter_storage_slot[row_adapter_index].astype(jnp.int32)

    def single_adapter(inputs):
        features, slot_indices = inputs
        down_projected_rows = adapter_down_weight[slot_indices].astype(jnp.float32)
        shrink = jnp.einsum('bf,bfa->ba', features.astype(jnp.float32), down_projected_rows).astype(jnp.bfloat16)
        up_projected_rows = adapter_up_weight[slot_indices].astype(jnp.float32)
        return jnp.einsum('ba,bad->bd', shrink.astype(jnp.float32), up_projected_rows)
    adapter_update = lax.map(single_adapter, (attention_result.reshape(block_list, ROWS_PER_SHARD, QUERY_HEADS * HEAD_WIDTH), row_storage_slot.reshape(block_list, ROWS_PER_SHARD))).reshape(DECODE_ROWS, OUTPUT_FEATURES)
    return (residual.astype(jnp.float32) + plain_output + adapter_update).astype(jnp.bfloat16)
```

```python
import functools
import math

import jax
import jax.numpy as jnp
from jax import lax
from jax.experimental import pallas as pl
from jax.experimental.pallas import tpu as pltpu
from jax.sharding import PartitionSpec as P

HEAD_WIDTH = 128
ROWS = 32
CTX = 128
REP = 32
TP = 16
CAP = 4
GROUP = 8
F32 = jnp.float32
BF16 = jnp.bfloat16
VMEM = pl.BlockSpec(memory_space=pltpu.VMEM)
ANY = pl.BlockSpec(memory_space=pl.ANY)


def iota(shape, dim):
    return lax.broadcasted_iota(jnp.int32, shape, dim)


def dot(a, b):
    return jnp.dot(a, b, preferred_element_type=F32)


def dot_t(a, b):
    return lax.dot_general(a, b, (((1,), (1,)), ((), ())), preferred_element_type=F32)


def one_hot(hit):
    return jnp.where(hit, 1.0, 0.0).astype(BF16)


def to_column(row):
    size = row.shape[1]
    eye = iota((size, size), 0) == iota((size, size), 1)
    return jnp.sum(jnp.where(eye, row, 0), axis=1, keepdims=True)


def to_row(column):
    size = column.shape[0]
    eye = iota((size, size), 0) == iota((size, size), 1)
    return jnp.sum(jnp.where(eye, column, 0), axis=0, keepdims=True)


def attend_kernel(
    q_ref, fresh_ref, lengths_ref, index_ref, table_ref, kv_hbm,
    attended_ref, send_ref, back_ref, kv_ref, sems,
):
    groups = ROWS // GROUP
    copies = [
        pltpu.make_async_copy(
            kv_hbm.at[pl.ds(g * GROUP, GROUP)], kv_ref.at[pl.ds(g * GROUP, GROUP)], sems.at[g]
        )
        for g in range(groups)
    ]
    for copy in copies:
        copy.start()

    table = table_ref[...]
    index = to_column(index_ref[...])
    size = table.shape[1]
    slot = jnp.sum(jnp.where(index == iota((ROWS, size), 1), table, 0), axis=1, keepdims=True)
    owner = slot // 4
    local = slot - owner * 4
    owner_row = to_row(owner)
    earlier = (owner == owner_row) & (iota((ROWS, ROWS), 0) > iota((ROWS, ROWS), 1))
    rank = jnp.sum(jnp.where(earlier, 1, 0), axis=1, keepdims=True)
    target = owner * CAP + rank
    back = iota((ROWS, 2 * REP * CAP), 1)
    for half in range(2):
        back_ref[half * ROWS:(half + 1) * ROWS, :] = one_hot(back == target * 2 + half)
    place = to_row(owner * 8 + rank)
    tags = one_hot(iota((ROWS, 2 * HEAD_WIDTH), 1) == local)
    rows_out = iota((8 * REP, ROWS), 0)
    place_tag = one_hot(rows_out == place + 4)
    place_row = one_hot(rows_out == place)

    lengths = to_column(lengths_ref[...])
    scale = 1.0 / math.sqrt(HEAD_WIDTH)
    row_at = iota((2 * GROUP, CTX), 0) % GROUP
    lane_at = iota((2 * GROUP, CTX), 1)
    for g in range(groups):
        at = slice(g * GROUP, (g + 1) * GROUP)
        q = q_ref[at, :].astype(F32)
        heads = jnp.concatenate([q[:, :HEAD_WIDTH], q[:, HEAD_WIDTH:]], axis=0)
        fresh = fresh_ref[at, :].astype(F32)
        fresh_key = jnp.concatenate([fresh[:, :HEAD_WIDTH]] * 2, axis=0)
        fresh_value = jnp.concatenate([fresh[:, HEAD_WIDTH:]] * 2, axis=0)
        own = jnp.sum(heads * fresh_key, axis=1, keepdims=True) * scale
        heads = heads.astype(BF16)
        live = lane_at < jnp.concatenate([lengths[at, :]] * 2, axis=0)
        copies[g].wait()
        scores = jnp.zeros((2 * GROUP, CTX), F32)
        for i in range(GROUP):
            part = dot_t(heads, kv_ref[g * GROUP + i, :, :HEAD_WIDTH])
            scores = jnp.where(row_at == i, part, scores)
        scores = jnp.where(live, scores * scale, -1e30)
        top = jnp.maximum(jnp.max(scores, axis=1, keepdims=True), own)
        weights = jnp.where(live, jnp.exp(scores - top), 0.0)
        own_weight = jnp.exp(own - top)
        denom = jnp.sum(weights, axis=1, keepdims=True) + own_weight
        probs = (weights / denom).astype(BF16)
        own_prob = (own_weight / denom).astype(BF16).astype(F32)
        mixed = jnp.zeros((2 * GROUP, HEAD_WIDTH), F32)
        for i in range(GROUP):
            part = dot(probs, kv_ref[g * GROUP + i, :, HEAD_WIDTH:])
            mixed = jnp.where(row_at == i, part, mixed)
        mixed = mixed + own_prob * fresh_value
        attended_ref[at, :] = jnp.concatenate([mixed[:GROUP], mixed[GROUP:]], axis=1).astype(BF16)
    send_ref[...] = (dot(place_row, attended_ref[...]) + dot(place_tag, tags)).astype(BF16)


def attend(queries, fresh, lengths, index, table, cache):
    return pl.pallas_call(
        attend_kernel,
        out_shape=(
            jax.ShapeDtypeStruct((ROWS, 2 * HEAD_WIDTH), BF16),
            jax.ShapeDtypeStruct((8 * REP, 2 * HEAD_WIDTH), BF16),
            jax.ShapeDtypeStruct((2 * ROWS, 2 * REP * CAP), BF16),
        ),
        in_specs=[VMEM] * 5 + [ANY],
        out_specs=(VMEM,) * 3,
        scratch_shapes=[
            pltpu.VMEM((ROWS, CTX, 2 * HEAD_WIDTH), BF16),
            pltpu.SemaphoreType.DMA((ROWS // GROUP,)),
        ],
        compiler_params=pltpu.CompilerParams(vmem_limit_bytes=16 * 2**20),
        name="attend",
    )(queries, fresh, lengths, index, table, cache)


def base_kernel(attended_ref, weight_ref, merged_ref):
    attended = attended_ref[...]
    for piece in range(TP):
        for half in range(2):
            at = (2 * piece + half) * 128
            merged_ref[piece, half * ROWS:(half + 1) * ROWS, :] = dot(
                attended, weight_ref[:, at:at + 128]
            ).astype(BF16)
        merged_ref[piece, 2 * ROWS:, :] = jnp.zeros((2 * ROWS, 128), BF16)


def base(attended, weight):
    return pl.pallas_call(
        base_kernel,
        out_shape=jax.ShapeDtypeStruct((TP, 4 * ROWS, 128), BF16),
        in_specs=[VMEM] * 2,
        out_specs=VMEM,
        compiler_params=pltpu.CompilerParams(vmem_limit_bytes=16 * 2**20),
        cost_estimate=pl.CostEstimate(
            flops=2 * 32 * 256 * 4096, bytes_accessed=3 * 2**20, transcendentals=0
        ),
        name="base",
    )(attended, weight)


def down_kernel(arrived_ref, down_ref, merged_in, merged_ref, mask_ref):
    arrived = arrived_ref[...]
    slots = REP * CAP
    slot = iota((slots, 8 * REP), 0)
    source = (slot // CAP) * 8 + slot % CAP
    at = iota((slots, 8 * REP), 1)
    features = dot(one_hot(at == source), arrived).astype(BF16)
    tags = dot(one_hot(at == source + 4), arrived[:, :128]).astype(BF16)
    spread = one_hot(iota((128, 256), 1) // 64 == iota((128, 256), 0))
    mask = dot(tags, spread)
    mask_ref[...] = mask.astype(BF16)
    product = dot_t(features, down_ref[...]) * mask
    product = product[:, :128] + product[:, 128:]
    product = product + pltpu.roll(product, 64, 1)
    low = iota((slots // 2, 128), 1) < 64
    part = jnp.where(low, product[:slots // 2], product[slots // 2:]).astype(BF16)
    for piece in range(TP):
        merged_ref[piece, 0:64, :] = merged_in[piece, 0:64, :]
        merged_ref[piece, 64:, :] = part


def down(arrived, down_weight, merged):
    return pl.pallas_call(
        down_kernel,
        out_shape=(
            jax.ShapeDtypeStruct(merged.shape, BF16),
            jax.ShapeDtypeStruct((REP * CAP, 256), BF16),
        ),
        in_specs=[VMEM] * 3,
        out_specs=(VMEM,) * 2,
        compiler_params=pltpu.CompilerParams(vmem_limit_bytes=16 * 2**20),
        name="down",
    )(arrived, down_weight, merged)


def up_kernel(merged_ref, mask_ref, up_ref, answer_ref, base_ref):
    total = merged_ref[0].astype(F32)
    for piece in range(1, TP):
        total = total + merged_ref[piece].astype(F32)
    base_ref[...] = total[:64]
    shrink = total[64:].astype(BF16).astype(F32)
    turned = pltpu.roll(shrink, 64, 1)
    low = iota(shrink.shape, 1) < 64
    shrink = jnp.concatenate(
        [jnp.where(low, shrink, turned), jnp.where(low, turned, shrink)], axis=0
    ).astype(BF16)
    spread = jnp.concatenate([shrink, shrink], axis=1) * mask_ref[...]
    answers = dot(spread, up_ref[...]).astype(BF16)
    slots = REP * CAP
    row = iota((2 * slots, slots), 0)
    at = iota((2 * slots, slots), 1)
    answer_ref[...] = (
        dot(one_hot(row == 2 * at), answers[:, :128])
        + dot(one_hot(row == 2 * at + 1), answers[:, 128:])
    ).astype(BF16)


def up(merged, mask, up_weight):
    return pl.pallas_call(
        up_kernel,
        out_shape=(
            jax.ShapeDtypeStruct((2 * REP * CAP, 128), BF16),
            jax.ShapeDtypeStruct((2 * ROWS, 128), F32),
        ),
        in_specs=[VMEM] * 3,
        out_specs=(VMEM,) * 2,
        compiler_params=pltpu.CompilerParams(vmem_limit_bytes=16 * 2**20),
        name="up",
    )(merged, mask, up_weight)


def final_kernel(returned_ref, back_ref, base_ref, residual_ref, out_ref):
    total = dot(back_ref[...], returned_ref[...]) + base_ref[...]
    total = jnp.concatenate([total[:ROWS], total[ROWS:]], axis=1)
    out_ref[...] = (residual_ref[...].astype(F32) + total).astype(BF16)


def final(returned, back, base_out, residual):
    return pl.pallas_call(
        final_kernel,
        out_shape=jax.ShapeDtypeStruct(residual.shape, BF16),
        in_specs=[VMEM] * 4,
        out_specs=VMEM,
        name="final",
    )(returned, back, base_out, residual)


def exchange(x, axis):
    return lax.all_to_all(x, axis, split_axis=0, concat_axis=0, tiled=True)


def on_device(
    queries,
    new_key_value,
    key_value_cache,
    lengths,
    residual,
    output_weight,
    row_adapter_index,
    adapter_storage_slot,
    adapter_down_weight,
    adapter_up_weight,
):
    attended, send, back = attend(
        queries,
        new_key_value.reshape(ROWS, 2 * HEAD_WIDTH),
        lengths.reshape(1, ROWS),
        row_adapter_index.reshape(1, ROWS),
        adapter_storage_slot.reshape(1, -1),
        key_value_cache.reshape(ROWS, CTX, 2 * HEAD_WIDTH),
    )
    arrived = exchange(send.reshape(REP, 8, 256), "rep").reshape(8 * REP, 256)
    merged = base(attended, output_weight)
    down_weight = jnp.swapaxes(adapter_down_weight, 1, 2).reshape(256, 256)
    merged, mask = down(arrived, down_weight, merged)
    merged = exchange(merged, "tp")
    answers, base_out = up(merged, mask, adapter_up_weight.reshape(256, 256))
    returned = exchange(answers.reshape(REP, 8, 128), "rep").reshape(8 * REP, 128)
    return final(returned, back, base_out, residual)


def solution(mesh):
    in_specs = (
        P("rep", "tp"),
        P("rep", "tp", None),
        P("rep", "tp", None, None),
        P("rep"),
        P("rep", "tp"),
        P("tp", None),
        P("rep"),
        P(),
        P("rep", "tp", None),
        P("rep", None, "tp"),
    )
    out_specs = P("rep", "tp")
    return jax.shard_map(
        on_device, mesh=mesh, in_specs=in_specs, out_specs=out_specs, check_vma=False
    )
```

```python
import functools
import math

import jax
import jax.numpy as jnp
from jax import lax
from jax.experimental import pallas as pl
from jax.experimental.pallas import tpu as pltpu
from jax.sharding import Mesh
from jax.sharding import PartitionSpec as P

HEAD_WIDTH = 128
ROWS = 32
CTX = 128
REP = 32
TP = 16
CAP = 4
GROUP = 8
F32 = jnp.float32
BF16 = jnp.bfloat16
VMEM = pl.BlockSpec(memory_space=pltpu.VMEM)
HBM = pl.BlockSpec(memory_space=pltpu.HBM)


def iota(shape, dim):
    return lax.broadcasted_iota(jnp.int32, shape, dim)


def dot(a, b):
    return jnp.dot(a, b, preferred_element_type=F32)


def dot_t(a, b):
    return lax.dot_general(a, b, (((1,), (1,)), ((), ())), preferred_element_type=F32)


def one_hot(hit):
    return jnp.where(hit, 1.0, 0.0).astype(BF16)


def to_column(row):
    size = row.shape[1]
    eye = iota((size, size), 0) == iota((size, size), 1)
    return jnp.sum(jnp.where(eye, row, 0), axis=1, keepdims=True)


def to_row(column):
    size = column.shape[0]
    eye = iota((size, size), 0) == iota((size, size), 1)
    return jnp.sum(jnp.where(eye, column, 0), axis=0, keepdims=True)


def attend_kernel(
    q_hbm, fresh_hbm, lengths_hbm, index_hbm, table_hbm, kv_hbm, weight_hbm, up_hbm,
    send_ref, back_ref, kept_ref, pack_ref,
    attended_ref, q_ref, fresh_ref, lengths_ref, index_ref, table_ref, kv_ref, weight_ref, small_sems, sems, weight_sem, up_sems,
):
    groups = ROWS // GROUP
    small = [
        pltpu.make_async_copy(src, dst, small_sems.at[i])
        for i, (src, dst) in enumerate((
            (index_hbm, index_ref),
            (table_hbm, table_ref),
            (lengths_hbm, lengths_ref),
            (q_hbm, q_ref),
            (fresh_hbm, fresh_ref),
        ))
    ]
    for copy in small:
        copy.start()
    copies = [
        pltpu.make_async_copy(
            kv_hbm.at[pl.ds(g * GROUP, GROUP)], kv_ref.at[pl.ds(g * GROUP, GROUP)], sems.at[g]
        )
        for g in range(groups)
    ]
    for copy in copies:
        copy.start()
    weight_copy = pltpu.make_async_copy(weight_hbm, weight_ref, weight_sem)
    weight_copy.start()
    half_rows = TP * ROWS
    up_copies = [
        pltpu.make_async_copy(
            up_hbm.at[:, pl.ds(half * 128, 128)],
            pack_ref.at[pl.ds(half_rows + half * 256, 256)],
            up_sems.at[half],
        )
        for half in range(2)
    ]
    for copy in up_copies:
        copy.start()
    for copy in small + copies:
        copy.wait()

    table = table_ref[...]
    index = to_column(index_ref[...])
    size = table.shape[1]
    slot = jnp.sum(jnp.where(index == iota((ROWS, size), 1), table, 0), axis=1, keepdims=True)
    owner = slot // 4
    local = slot - owner * 4
    owner_row = to_row(owner)
    earlier = (owner == owner_row) & (iota((ROWS, ROWS), 0) > iota((ROWS, ROWS), 1))
    rank = jnp.sum(jnp.where(earlier, 1, 0), axis=1, keepdims=True)
    target = owner * CAP + rank
    back = iota((ROWS, 2 * REP * CAP), 1)
    for half in range(2):
        back_ref[half * ROWS:(half + 1) * ROWS, :] = one_hot(back == target * 2 + half)
    place = to_row(owner * 8 + rank)
    tags = one_hot(iota((ROWS, 2 * HEAD_WIDTH), 1) == local)
    rows_out = iota((8 * REP, ROWS), 0)
    place_tag = one_hot(rows_out == place + 4)
    place_row = one_hot(rows_out == place)

    lengths = to_column(lengths_ref[...])
    scale = 1.0 / math.sqrt(HEAD_WIDTH)
    row_at = iota((2 * GROUP, CTX), 0) % GROUP
    lane_at = iota((2 * GROUP, CTX), 1)
    for g in range(groups):
        at = slice(g * GROUP, (g + 1) * GROUP)
        q = q_ref[at, :].astype(F32)
        heads = jnp.concatenate([q[:, :HEAD_WIDTH], q[:, HEAD_WIDTH:]], axis=0)
        fresh = fresh_ref[at, :].astype(F32)
        fresh_key = jnp.concatenate([fresh[:, :HEAD_WIDTH]] * 2, axis=0)
        fresh_value = jnp.concatenate([fresh[:, HEAD_WIDTH:]] * 2, axis=0)
        own = jnp.sum(heads * fresh_key, axis=1, keepdims=True) * scale
        heads = heads.astype(BF16)
        live = lane_at < jnp.concatenate([lengths[at, :]] * 2, axis=0)
        scores = jnp.zeros((2 * GROUP, CTX), F32)
        for i in range(GROUP):
            part = dot_t(heads, kv_ref[g * GROUP + i, :, :HEAD_WIDTH])
            scores = jnp.where(row_at == i, part, scores)
        scores = jnp.where(live, scores * scale, -1e30)
        top = jnp.maximum(jnp.max(scores, axis=1, keepdims=True), own)
        weights = jnp.where(live, jnp.exp(scores - top), 0.0)
        own_weight = jnp.exp(own - top)
        denom = jnp.sum(weights, axis=1, keepdims=True) + own_weight
        probs = (weights / denom).astype(BF16)
        own_prob = (own_weight / denom).astype(BF16).astype(F32)
        mixed = jnp.zeros((2 * GROUP, HEAD_WIDTH), F32)
        for i in range(GROUP):
            part = dot(probs, kv_ref[g * GROUP + i, :, HEAD_WIDTH:])
            mixed = jnp.where(row_at == i, part, mixed)
        mixed = mixed + own_prob * fresh_value
        attended_ref[at, :] = jnp.concatenate([mixed[:GROUP], mixed[GROUP:]], axis=1).astype(BF16)
    attended = attended_ref[...]
    weight_copy.wait()
    mine = lax.axis_index("near")
    for piece in range(TP):
        for ref, half in ((pack_ref, 1 - mine), (kept_ref, mine)):
            at = pl.multiple_of((2 * piece + half) * 128, 128)
            ref[piece * ROWS:(piece + 1) * ROWS, :] = dot(
                attended, weight_ref[:, pl.ds(at, 128)]
            ).astype(BF16)
    send_ref[...] = (dot(place_row, attended_ref[...]) + dot(place_tag, tags)).astype(BF16)
    for copy in up_copies:
        copy.wait()


def attend(queries, fresh, lengths, index, table, cache, weight, up_weight):
    return pl.pallas_call(
        attend_kernel,
        out_shape=(
            jax.ShapeDtypeStruct((8 * REP, 2 * HEAD_WIDTH), BF16),
            jax.ShapeDtypeStruct((2 * ROWS, 2 * REP * CAP), BF16),
            jax.ShapeDtypeStruct((TP * ROWS, 128), BF16),
            jax.ShapeDtypeStruct((TP * ROWS + 512, 128), BF16),
        ),
        in_specs=[HBM] * 8,
        out_specs=(VMEM,) * 4,
        scratch_shapes=[
            pltpu.VMEM(queries.shape, BF16),
            pltpu.VMEM(queries.shape, BF16),
            pltpu.VMEM(fresh.shape, BF16),
            pltpu.VMEM(lengths.shape, jnp.int32),
            pltpu.VMEM(index.shape, jnp.int32),
            pltpu.VMEM(table.shape, jnp.int32),
            pltpu.VMEM((ROWS, CTX, 2 * HEAD_WIDTH), BF16),
            pltpu.VMEM(weight.shape, BF16),
            pltpu.SemaphoreType.DMA((5,)),
            pltpu.SemaphoreType.DMA((ROWS // GROUP,)),
            pltpu.SemaphoreType.DMA,
            pltpu.SemaphoreType.DMA((2,)),
        ],
        compiler_params=pltpu.CompilerParams(vmem_limit_bytes=56 * 2**20),
        name="attend",
    )(queries, fresh, lengths, index, table, cache, weight, up_weight)


def down_kernel(arrived_ref, down_ref, kept_ref, near_ref, merged_ref, mask_ref):
    arrived = arrived_ref[...]
    slots = REP * CAP
    slot = iota((slots, 8 * REP), 0)
    source = (slot % 64 // 2) * 8 + slot // 64 * 2 + slot % 2
    at = iota((slots, 8 * REP), 1)
    features = dot(one_hot(at == source), arrived).astype(BF16)
    tags = dot(one_hot(at == source + 4), arrived[:, :128]).astype(BF16)
    spread = one_hot(iota((128, 256), 1) // 64 == iota((128, 256), 0))
    mask = dot(tags, spread)
    mask_ref[...] = mask.astype(BF16)
    product = dot_t(features, down_ref[...]) * mask
    product = product[:, :128] + product[:, 128:]
    product = product + pltpu.roll(product, 64, 1)
    low = iota((32, 128), 1) < 64
    parts = [
        jnp.where(low, product[64 * p:64 * p + 32], product[64 * p + 32:64 * p + 64]).astype(BF16)
        for p in range(2)
    ]
    for piece in range(TP):
        at = slice(piece * ROWS, (piece + 1) * ROWS)
        merged_ref[piece, :ROWS, :] = (
            kept_ref[at, :].astype(F32) + near_ref[at, :].astype(F32)
        ).astype(BF16)
        merged_ref[piece, ROWS:, :] = parts[piece % 2]


def down(arrived, down_weight, kept, near):
    return pl.pallas_call(
        down_kernel,
        out_shape=(
            jax.ShapeDtypeStruct((TP, 2 * ROWS, 128), BF16),
            jax.ShapeDtypeStruct((REP * CAP, 256), BF16),
        ),
        in_specs=[VMEM] * 4,
        out_specs=(VMEM,) * 2,
        compiler_params=pltpu.CompilerParams(vmem_limit_bytes=8 * 2**20),
        name="down",
    )(arrived, down_weight, kept, near)


def up_kernel(merged_ref, mask_ref, up_ref, near_ref, answer_ref, base_ref):
    mine = lax.axis_index("near")
    sums = []
    for p in range(2):
        total = merged_ref[p].astype(F32)
        for piece in range(p + 2, TP, 2):
            total = total + merged_ref[piece].astype(F32)
        base_ref[p * ROWS:(p + 1) * ROWS, :] = total[:ROWS]
        sums.append(total[ROWS:])
    shrink = (sums[0] + sums[1]).astype(BF16).astype(F32)
    turned = pltpu.roll(shrink, 64, 1)
    low = iota(shrink.shape, 1) < 64
    shrink = jnp.concatenate(
        [jnp.where(low, shrink, turned), jnp.where(low, turned, shrink)], axis=0
    ).astype(BF16)
    mask = mask_ref[pl.ds(pl.multiple_of(mine * 64, 64), 64), :]
    spread = jnp.concatenate([shrink, shrink], axis=1) * mask
    row = iota((8 * REP, 64), 0)
    at = iota((8 * REP, 64), 1)
    first = (at // 2) * 8 + (at % 2) * 2
    total = jnp.zeros((8 * REP, 128), F32)
    for half in range(2):
        near_at = TP * ROWS + half * 256
        for up_half, side in (
            (up_ref[:, half * 128:(half + 1) * 128], mine),
            (near_ref[near_at:near_at + 256, :], 1 - mine),
        ):
            answers = dot(spread, up_half).astype(BF16)
            total = total + dot(one_hot(row == first + side * 4 + half), answers)
    answer_ref[...] = total.astype(BF16)


def up(merged, mask, up_weight, near):
    return pl.pallas_call(
        up_kernel,
        out_shape=(
            jax.ShapeDtypeStruct((8 * REP, 128), BF16),
            jax.ShapeDtypeStruct((2 * ROWS, 128), F32),
        ),
        in_specs=[VMEM] * 4,
        out_specs=(VMEM,) * 2,
        compiler_params=pltpu.CompilerParams(vmem_limit_bytes=8 * 2**20),
        name="up",
    )(merged, mask, up_weight, near)


def final_kernel(returned_ref, back_ref, base_ref, residual_ref, out_ref):
    total = dot(back_ref[...], returned_ref[...]) + base_ref[...]
    total = jnp.concatenate([total[:ROWS], total[ROWS:]], axis=1)
    out_ref[...] = (residual_ref[...].astype(F32) + total).astype(BF16)


def final(returned, back, base_out, residual):
    return pl.pallas_call(
        final_kernel,
        out_shape=jax.ShapeDtypeStruct(residual.shape, BF16),
        in_specs=[VMEM] * 4,
        out_specs=VMEM,
        compiler_params=pltpu.CompilerParams(vmem_limit_bytes=8 * 2**20),
        name="final",
    )(returned, back, base_out, residual)


def exchange(x, axis):
    return lax.all_to_all(x, axis, split_axis=0, concat_axis=0, tiled=True)


def swap_near(x):
    return lax.ppermute(x, "near", [(0, 1), (1, 0)])


def on_device(
    queries,
    new_key_value,
    key_value_cache,
    lengths,
    residual,
    output_weight,
    row_adapter_index,
    adapter_storage_slot,
    adapter_down_weight,
    adapter_up_weight,
):
    up_weight = adapter_up_weight.reshape(256, 256)
    send, back, kept, pack = attend(
        queries,
        new_key_value.reshape(ROWS, 2 * HEAD_WIDTH),
        lengths.reshape(1, ROWS),
        row_adapter_index.reshape(1, ROWS),
        adapter_storage_slot.reshape(1, -1),
        key_value_cache.reshape(ROWS, CTX, 2 * HEAD_WIDTH),
        output_weight,
        up_weight,
    )
    arrived = exchange(send.reshape(REP, 8, 256), "rep").reshape(8 * REP, 256)
    near = swap_near(pack)
    down_weight = jnp.swapaxes(adapter_down_weight, 1, 2).reshape(256, 256)
    merged, mask = down(arrived, down_weight, kept, near)
    merged = exchange(merged, ("far", "near"))
    answers, base_out = up(merged, mask, up_weight, near)
    returned = exchange(answers.reshape(2 * REP, 4, 128), ("rep", "near")).reshape(8 * REP, 128)
    return final(returned, back, base_out, residual)


def solution(mesh):
    mesh = Mesh(mesh.devices.reshape(REP, TP // 2, 2), ("rep", "far", "near"))
    tp = ("far", "near")
    in_specs = (
        P("rep", tp),
        P("rep", tp, None),
        P("rep", tp, None, None),
        P("rep"),
        P("rep", tp),
        P(tp, None),
        P("rep"),
        P(),
        P("rep", tp, None),
        P("rep", None, tp),
    )
    return jax.shard_map(
        on_device, mesh=mesh, in_specs=in_specs, out_specs=P("rep", tp), check_vma=False
    )
```

```python
import functools
import math

import jax
import jax.numpy as jnp
from jax import lax
from jax.experimental import pallas as pl
from jax.experimental.pallas import tpu as pltpu
from jax.sharding import Mesh
from jax.sharding import PartitionSpec as P

HEAD_WIDTH = 128
ROWS = 32
CTX = 128
REP = 32
TP = 16
CAP = 4
GROUP = 8
F32 = jnp.float32
BF16 = jnp.bfloat16
VMEM = pl.BlockSpec(memory_space=pltpu.VMEM)
HBM = pl.BlockSpec(memory_space=pltpu.HBM)


def iota(shape, dim):
    return lax.broadcasted_iota(jnp.int32, shape, dim)


def dot(a, b):
    return jnp.dot(a, b, preferred_element_type=F32)


def dot_t(a, b):
    return lax.dot_general(a, b, (((1,), (1,)), ((), ())), preferred_element_type=F32)


def one_hot(hit):
    return jnp.where(hit, 1.0, 0.0).astype(BF16)


def to_column(row):
    size = row.shape[1]
    eye = iota((size, size), 0) == iota((size, size), 1)
    return jnp.sum(jnp.where(eye, row, 0), axis=1, keepdims=True)


def to_row(column):
    size = column.shape[0]
    eye = iota((size, size), 0) == iota((size, size), 1)
    return jnp.sum(jnp.where(eye, column, 0), axis=0, keepdims=True)


def attend_kernel(
    q_hbm, fresh_hbm, lengths_hbm, index_hbm, table_hbm, kv_hbm, weight_hbm, up_hbm,
    send_ref, back_ref, kept_ref, pack_ref,
    attended_ref, q_ref, fresh_ref, lengths_ref, index_ref, table_ref, kv_ref, weight_ref, small_sems, sems, weight_sem, up_sems,
):
    groups = ROWS // GROUP
    small = [
        pltpu.make_async_copy(src, dst, small_sems.at[i])
        for i, (src, dst) in enumerate((
            (index_hbm, index_ref),
            (table_hbm, table_ref),
            (lengths_hbm, lengths_ref),
            (q_hbm, q_ref),
            (fresh_hbm, fresh_ref),
        ))
    ]
    for copy in small:
        copy.start()
    copies = [
        pltpu.make_async_copy(
            kv_hbm.at[pl.ds(g * GROUP, GROUP)], kv_ref.at[pl.ds(g * GROUP, GROUP)], sems.at[g]
        )
        for g in range(groups)
    ]
    for copy in copies:
        copy.start()
    weight_copy = pltpu.make_async_copy(weight_hbm, weight_ref, weight_sem)
    weight_copy.start()
    half_rows = TP * ROWS
    up_copies = [
        pltpu.make_async_copy(
            up_hbm.at[:, pl.ds(half * 128, 128)],
            pack_ref.at[pl.ds(half_rows + half * 256, 256)],
            up_sems.at[half],
        )
        for half in range(2)
    ]
    for copy in up_copies:
        copy.start()
    for copy in small:
        copy.wait()

    table = table_ref[...]
    index = to_column(index_ref[...])
    size = table.shape[1]
    slot = jnp.sum(jnp.where(index == iota((ROWS, size), 1), table, 0), axis=1, keepdims=True)
    owner = slot // 4
    local = slot - owner * 4
    owner_row = to_row(owner)
    earlier = (owner == owner_row) & (iota((ROWS, ROWS), 0) > iota((ROWS, ROWS), 1))
    rank = jnp.sum(jnp.where(earlier, 1, 0), axis=1, keepdims=True)
    target = owner * CAP + rank
    back = iota((ROWS, 2 * REP * CAP), 1)
    for half in range(2):
        back_ref[half * ROWS:(half + 1) * ROWS, :] = one_hot(back == target * 2 + half)
    place = to_row(owner * 8 + rank)
    tags = one_hot(iota((ROWS, 2 * HEAD_WIDTH), 1) == local)
    rows_out = iota((8 * REP, ROWS), 0)
    place_tag = one_hot(rows_out == place + 4)
    place_row = one_hot(rows_out == place)

    lengths = to_column(lengths_ref[...])
    for copy in copies:
        copy.wait()
    scale = 1.0 / math.sqrt(HEAD_WIDTH)
    q = q_ref[...].astype(F32)
    heads = jnp.concatenate([q[:, :HEAD_WIDTH], q[:, HEAD_WIDTH:]], axis=0)
    fresh = fresh_ref[...].astype(F32)
    fresh_key = jnp.concatenate([fresh[:, :HEAD_WIDTH]] * 2, axis=0)
    own = jnp.sum(heads * fresh_key, axis=1, keepdims=True) * scale
    heads = jnp.concatenate([heads, heads], axis=0).astype(BF16)
    column = iota((CTX, 4 * ROWS), 1) % ROWS
    turned = jnp.zeros((CTX, 4 * ROWS), F32)
    for r in range(ROWS):
        turned = jnp.where(column == r, dot_t(kv_ref[r, :, :HEAD_WIDTH], heads), turned)
    live = iota((2 * ROWS, CTX), 1) < jnp.concatenate([lengths] * 2, axis=0)
    scores = jnp.where(live, turned.T[:2 * ROWS] * scale, -1e30)
    top = jnp.maximum(jnp.max(scores, axis=1, keepdims=True), own)
    weights = jnp.where(live, jnp.exp(scores - top), 0.0)
    own_weight = jnp.exp(own - top)
    denom = jnp.sum(weights, axis=1, keepdims=True) + own_weight
    probs = weights / denom
    own_prob = (own_weight / denom).astype(BF16).astype(F32)
    row_at = iota((2 * GROUP, CTX), 0) % GROUP
    for g in range(groups):
        at = slice(g * GROUP, (g + 1) * GROUP)
        both = slice(ROWS + g * GROUP, ROWS + (g + 1) * GROUP)
        part_probs = jnp.concatenate([probs[at], probs[both]], axis=0).astype(BF16)
        mixed = jnp.zeros((2 * GROUP, HEAD_WIDTH), F32)
        for i in range(GROUP):
            part = dot(part_probs, kv_ref[g * GROUP + i, :, HEAD_WIDTH:])
            mixed = jnp.where(row_at == i, part, mixed)
        value = fresh[at, HEAD_WIDTH:]
        attended_ref[at, :] = jnp.concatenate(
            [mixed[:GROUP] + own_prob[at] * value, mixed[GROUP:] + own_prob[both] * value], axis=1
        ).astype(BF16)
    attended = attended_ref[...]
    weight_copy.wait()
    mine = lax.axis_index("near")
    for piece in range(TP):
        for ref, half in ((pack_ref, 1 - mine), (kept_ref, mine)):
            at = pl.multiple_of((2 * piece + half) * 128, 128)
            ref[piece * ROWS:(piece + 1) * ROWS, :] = dot(
                attended, weight_ref[:, pl.ds(at, 128)]
            ).astype(BF16)
    send_ref[...] = (dot(place_row, attended_ref[...]) + dot(place_tag, tags)).astype(BF16)
    for copy in up_copies:
        copy.wait()


def attend(queries, fresh, lengths, index, table, cache, weight, up_weight):
    return pl.pallas_call(
        attend_kernel,
        out_shape=(
            jax.ShapeDtypeStruct((8 * REP, 2 * HEAD_WIDTH), BF16),
            jax.ShapeDtypeStruct((2 * ROWS, 2 * REP * CAP), BF16),
            jax.ShapeDtypeStruct((TP * ROWS, 128), BF16),
            jax.ShapeDtypeStruct((TP * ROWS + 512, 128), BF16),
        ),
        in_specs=[HBM] * 8,
        out_specs=(VMEM,) * 4,
        scratch_shapes=[
            pltpu.VMEM(queries.shape, BF16),
            pltpu.VMEM(queries.shape, BF16),
            pltpu.VMEM(fresh.shape, BF16),
            pltpu.VMEM(lengths.shape, jnp.int32),
            pltpu.VMEM(index.shape, jnp.int32),
            pltpu.VMEM(table.shape, jnp.int32),
            pltpu.VMEM((ROWS, CTX, 2 * HEAD_WIDTH), BF16),
            pltpu.VMEM(weight.shape, BF16),
            pltpu.SemaphoreType.DMA((5,)),
            pltpu.SemaphoreType.DMA((ROWS // GROUP,)),
            pltpu.SemaphoreType.DMA,
            pltpu.SemaphoreType.DMA((2,)),
        ],
        compiler_params=pltpu.CompilerParams(vmem_limit_bytes=12 * 2**20),
        name="attend",
    )(*[pltpu.with_memory_space_constraint(x, pltpu.HBM) for x in (queries, fresh, lengths, index, table, cache, weight, up_weight)])


def down_kernel(arrived_ref, down_ref, kept_ref, near_ref, merged_ref, mask_ref):
    arrived = arrived_ref[...]
    slots = REP * CAP
    slot = iota((slots, 8 * REP), 0)
    source = (slot % 64 // 2) * 8 + slot // 64 * 2 + slot % 2
    at = iota((slots, 8 * REP), 1)
    features = dot(one_hot(at == source), arrived).astype(BF16)
    tags = dot(one_hot(at == source + 4), arrived[:, :128]).astype(BF16)
    spread = one_hot(iota((128, 256), 1) // 64 == iota((128, 256), 0))
    mask = dot(tags, spread)
    mask_ref[...] = mask.astype(BF16)
    product = dot_t(features, down_ref[...]) * mask
    product = product[:, :128] + product[:, 128:]
    product = product + pltpu.roll(product, 64, 1)
    low = iota((32, 128), 1) < 64
    parts = [
        jnp.where(low, product[64 * p:64 * p + 32], product[64 * p + 32:64 * p + 64]).astype(BF16)
        for p in range(2)
    ]
    for piece in range(TP):
        at = slice(piece * ROWS, (piece + 1) * ROWS)
        merged_ref[piece, :ROWS, :] = (
            kept_ref[at, :].astype(F32) + near_ref[at, :].astype(F32)
        ).astype(BF16)
        merged_ref[piece, ROWS:, :] = parts[piece % 2]


def down(arrived, down_weight, kept, near):
    return pl.pallas_call(
        down_kernel,
        out_shape=(
            jax.ShapeDtypeStruct((TP, 2 * ROWS, 128), BF16),
            jax.ShapeDtypeStruct((REP * CAP, 256), BF16),
        ),
        in_specs=[VMEM] * 4,
        out_specs=(VMEM,) * 2,
        compiler_params=pltpu.CompilerParams(vmem_limit_bytes=8 * 2**20),
        name="down",
    )(arrived, down_weight, kept, near)


def up_kernel(merged_ref, mask_ref, up_ref, near_ref, answer_ref, base_ref):
    mine = lax.axis_index("near")
    sums = []
    for p in range(2):
        total = merged_ref[p].astype(F32)
        for piece in range(p + 2, TP, 2):
            total = total + merged_ref[piece].astype(F32)
        base_ref[p * ROWS:(p + 1) * ROWS, :] = total[:ROWS]
        sums.append(total[ROWS:])
    shrink = (sums[0] + sums[1]).astype(BF16).astype(F32)
    turned = pltpu.roll(shrink, 64, 1)
    low = iota(shrink.shape, 1) < 64
    shrink = jnp.concatenate(
        [jnp.where(low, shrink, turned), jnp.where(low, turned, shrink)], axis=0
    ).astype(BF16)
    mask = mask_ref[pl.ds(pl.multiple_of(mine * 64, 64), 64), :]
    spread = jnp.concatenate([shrink, shrink], axis=1) * mask
    row = iota((8 * REP, 64), 0)
    at = iota((8 * REP, 64), 1)
    first = (at // 2) * 8 + (at % 2) * 2
    total = jnp.zeros((8 * REP, 128), F32)
    for half in range(2):
        near_at = TP * ROWS + half * 256
        for up_half, side in (
            (up_ref[:, half * 128:(half + 1) * 128], mine),
            (near_ref[near_at:near_at + 256, :], 1 - mine),
        ):
            answers = dot(spread, up_half).astype(BF16)
            total = total + dot(one_hot(row == first + side * 4 + half), answers)
    answer_ref[...] = total.astype(BF16)


def up(merged, mask, up_weight, near):
    return pl.pallas_call(
        up_kernel,
        out_shape=(
            jax.ShapeDtypeStruct((8 * REP, 128), BF16),
            jax.ShapeDtypeStruct((2 * ROWS, 128), F32),
        ),
        in_specs=[VMEM] * 4,
        out_specs=(VMEM,) * 2,
        compiler_params=pltpu.CompilerParams(vmem_limit_bytes=8 * 2**20),
        name="up",
    )(merged, mask, up_weight, near)


def final_kernel(returned_ref, back_ref, base_ref, residual_ref, out_ref):
    total = dot(back_ref[...], returned_ref[...]) + base_ref[...]
    total = jnp.concatenate([total[:ROWS], total[ROWS:]], axis=1)
    out_ref[...] = (residual_ref[...].astype(F32) + total).astype(BF16)


def final(returned, back, base_out, residual):
    return pl.pallas_call(
        final_kernel,
        out_shape=jax.ShapeDtypeStruct(residual.shape, BF16),
        in_specs=[VMEM] * 4,
        out_specs=VMEM,
        compiler_params=pltpu.CompilerParams(vmem_limit_bytes=8 * 2**20),
        name="final",
    )(returned, back, base_out, residual)


def exchange(x, axis):
    return lax.all_to_all(x, axis, split_axis=0, concat_axis=0, tiled=True)


def swap_near(x):
    return lax.ppermute(x, "near", [(0, 1), (1, 0)])


def on_device(
    queries,
    new_key_value,
    key_value_cache,
    lengths,
    residual,
    output_weight,
    row_adapter_index,
    adapter_storage_slot,
    adapter_down_weight,
    adapter_up_weight,
):
    up_weight = adapter_up_weight.reshape(256, 256)
    send, back, kept, pack = attend(
        queries,
        new_key_value.reshape(ROWS, 2 * HEAD_WIDTH),
        lengths.reshape(1, ROWS),
        row_adapter_index.reshape(1, ROWS),
        adapter_storage_slot.reshape(1, -1),
        key_value_cache.reshape(ROWS, CTX, 2 * HEAD_WIDTH),
        output_weight,
        up_weight,
    )
    arrived = exchange(send.reshape(REP, 8, 256), "rep").reshape(8 * REP, 256)
    near = swap_near(pack)
    down_weight = jnp.swapaxes(adapter_down_weight, 1, 2).reshape(256, 256)
    merged, mask = down(arrived, down_weight, kept, near)
    merged = exchange(merged, ("far", "near"))
    answers, base_out = up(merged, mask, up_weight, near)
    returned = exchange(answers.reshape(2 * REP, 4, 128), ("rep", "near")).reshape(8 * REP, 128)
    return final(returned, back, base_out, residual)


def solution(mesh):
    mesh = Mesh(mesh.devices.reshape(REP, TP // 2, 2), ("rep", "far", "near"))
    tp = ("far", "near")
    in_specs = (
        P("rep", tp),
        P("rep", tp, None),
        P("rep", tp, None, None),
        P("rep"),
        P("rep", tp),
        P(tp, None),
        P("rep"),
        P(),
        P("rep", tp, None),
        P("rep", None, tp),
    )
    return jax.shard_map(
        on_device, mesh=mesh, in_specs=in_specs, out_specs=P("rep", tp), check_vma=False
    )
```

```python
import functools
import math

import jax
import jax.numpy as jnp
from jax import lax
from jax.experimental import pallas as pl
from jax.experimental.pallas import tpu as pltpu
from jax.sharding import Mesh
from jax.sharding import PartitionSpec as P

HEAD_WIDTH = 128
ROWS = 32
CTX = 128
REP = 32
TP = 16
CAP = 4
GROUP = 8
F32 = jnp.float32
BF16 = jnp.bfloat16
VMEM = pl.BlockSpec(memory_space=pltpu.VMEM)
HBM = pl.BlockSpec(memory_space=pltpu.HBM)


def iota(shape, dim):
    return lax.broadcasted_iota(jnp.int32, shape, dim)


def dot(a, b):
    return jnp.dot(a, b, preferred_element_type=F32)


def dot_t(a, b):
    return lax.dot_general(a, b, (((1,), (1,)), ((), ())), preferred_element_type=F32)


def one_hot(hit):
    return jnp.where(hit, 1.0, 0.0).astype(BF16)


def to_column(row):
    size = row.shape[1]
    eye = iota((size, size), 0) == iota((size, size), 1)
    return jnp.sum(jnp.where(eye, row, 0), axis=1, keepdims=True)


def to_row(column):
    size = column.shape[0]
    eye = iota((size, size), 0) == iota((size, size), 1)
    return jnp.sum(jnp.where(eye, column, 0), axis=0, keepdims=True)


def attend_kernel(
    q_hbm, fresh_hbm, lengths_hbm, index_hbm, table_hbm, kv_hbm, weight_hbm, up_hbm,
    send_ref, back_ref, kept_ref, pack_ref,
    attended_ref, q_ref, fresh_ref, lengths_ref, index_ref, table_ref, kv_ref, weight_ref, small_sems, sems, weight_sem, up_sems,
):
    groups = ROWS // GROUP
    small = [
        pltpu.make_async_copy(src, dst, small_sems.at[i])
        for i, (src, dst) in enumerate((
            (index_hbm, index_ref),
            (table_hbm, table_ref),
            (lengths_hbm, lengths_ref),
            (q_hbm, q_ref),
            (fresh_hbm, fresh_ref),
        ))
    ]
    for copy in small:
        copy.start()
    copies = [
        pltpu.make_async_copy(
            kv_hbm.at[pl.ds(g * GROUP, GROUP)], kv_ref.at[pl.ds(g * GROUP, GROUP)], sems.at[g]
        )
        for g in range(groups)
    ]
    for copy in copies:
        copy.start()
    weight_copy = pltpu.make_async_copy(weight_hbm, weight_ref, weight_sem)
    weight_copy.start()
    half_rows = TP * ROWS
    up_copies = [
        pltpu.make_async_copy(
            up_hbm.at[:, pl.ds(half * 128, 128)],
            pack_ref.at[pl.ds(half_rows + half * 256, 256)],
            up_sems.at[half],
        )
        for half in range(2)
    ]
    for copy in up_copies:
        copy.start()
    for copy in small:
        copy.wait()

    table = table_ref[...]
    index = to_column(index_ref[...])
    size = table.shape[1]
    slot = jnp.sum(jnp.where(index == iota((ROWS, size), 1), table, 0), axis=1, keepdims=True)
    owner = slot // 4
    local = slot - owner * 4
    owner_row = to_row(owner)
    earlier = (owner == owner_row) & (iota((ROWS, ROWS), 0) > iota((ROWS, ROWS), 1))
    rank = jnp.sum(jnp.where(earlier, 1, 0), axis=1, keepdims=True)
    target = owner * CAP + rank
    back = iota((ROWS, 2 * REP * CAP), 1)
    for half in range(2):
        back_ref[half * ROWS:(half + 1) * ROWS, :] = one_hot(back == target * 2 + half)
    place = to_row(owner * 8 + rank)
    tags = one_hot(iota((ROWS, 2 * HEAD_WIDTH), 1) == local)
    rows_out = iota((8 * REP, ROWS), 0)
    place_tag = one_hot(rows_out == place + 4)
    place_row = one_hot(rows_out == place)

    lengths = to_column(lengths_ref[...])
    for copy in copies:
        copy.wait()
    scale = 1.0 / math.sqrt(HEAD_WIDTH)
    q = q_ref[...].astype(F32)
    heads = jnp.concatenate([q[:, :HEAD_WIDTH], q[:, HEAD_WIDTH:]], axis=0)
    fresh = fresh_ref[...].astype(F32)
    fresh_key = jnp.concatenate([fresh[:, :HEAD_WIDTH]] * 2, axis=0)
    own = jnp.sum(heads * fresh_key, axis=1, keepdims=True) * scale
    empty = jnp.zeros_like(heads)
    heads = jnp.concatenate(
        [jnp.concatenate([heads, empty], axis=1), jnp.concatenate([empty, heads], axis=1)], axis=0
    ).astype(BF16)
    column = iota((CTX, 4 * ROWS), 1)
    column = column % ROWS - column // (2 * ROWS) * (ROWS // 2)
    turned = jnp.zeros((CTX, 4 * ROWS), F32)
    for r in range(ROWS // 2):
        keys = jnp.concatenate(
            [kv_ref[r, :, :HEAD_WIDTH], kv_ref[r + ROWS // 2, :, :HEAD_WIDTH]], axis=1
        )
        turned = jnp.where(column == r, dot_t(keys, heads), turned)
    turned = turned.T
    early = iota((2 * ROWS, CTX), 0) % ROWS < ROWS // 2
    turned = jnp.where(early, turned[:2 * ROWS], turned[2 * ROWS:])
    live = iota((2 * ROWS, CTX), 1) < jnp.concatenate([lengths] * 2, axis=0)
    scores = jnp.where(live, turned * scale, -1e30)
    top = jnp.maximum(jnp.max(scores, axis=1, keepdims=True), own)
    weights = jnp.where(live, jnp.exp(scores - top), 0.0)
    own_weight = jnp.exp(own - top)
    denom = jnp.sum(weights, axis=1, keepdims=True) + own_weight
    probs = weights / denom
    own_prob = (own_weight / denom).astype(BF16).astype(F32)
    row_at = iota((2 * GROUP, CTX), 0) % GROUP
    for g in range(groups):
        at = slice(g * GROUP, (g + 1) * GROUP)
        both = slice(ROWS + g * GROUP, ROWS + (g + 1) * GROUP)
        part_probs = jnp.concatenate([probs[at], probs[both]], axis=0)
        spread = jnp.concatenate(
            [jnp.where(row_at == i, part_probs, 0.0) for i in range(GROUP)], axis=1
        ).astype(BF16)
        values = kv_ref[g * GROUP:(g + 1) * GROUP, :, HEAD_WIDTH:].reshape(GROUP * CTX, HEAD_WIDTH)
        mixed = dot(spread, values)
        value = fresh[at, HEAD_WIDTH:]
        attended_ref[at, :] = jnp.concatenate(
            [mixed[:GROUP] + own_prob[at] * value, mixed[GROUP:] + own_prob[both] * value], axis=1
        ).astype(BF16)
    attended = attended_ref[...]
    weight_copy.wait()
    mine = lax.axis_index("near")
    for piece in range(TP):
        for ref, half in ((pack_ref, 1 - mine), (kept_ref, mine)):
            at = pl.multiple_of((2 * piece + half) * 128, 128)
            ref[piece * ROWS:(piece + 1) * ROWS, :] = dot(
                attended, weight_ref[:, pl.ds(at, 128)]
            ).astype(BF16)
    send_ref[...] = (dot(place_row, attended_ref[...]) + dot(place_tag, tags)).astype(BF16)
    for copy in up_copies:
        copy.wait()


def attend(queries, fresh, lengths, index, table, cache, weight, up_weight):
    return pl.pallas_call(
        attend_kernel,
        out_shape=(
            jax.ShapeDtypeStruct((8 * REP, 2 * HEAD_WIDTH), BF16),
            jax.ShapeDtypeStruct((2 * ROWS, 2 * REP * CAP), BF16),
            jax.ShapeDtypeStruct((TP * ROWS, 128), BF16),
            jax.ShapeDtypeStruct((TP * ROWS + 512, 128), BF16),
        ),
        in_specs=[HBM] * 8,
        out_specs=(VMEM,) * 4,
        scratch_shapes=[
            pltpu.VMEM(queries.shape, BF16),
            pltpu.VMEM(queries.shape, BF16),
            pltpu.VMEM(fresh.shape, BF16),
            pltpu.VMEM(lengths.shape, jnp.int32),
            pltpu.VMEM(index.shape, jnp.int32),
            pltpu.VMEM(table.shape, jnp.int32),
            pltpu.VMEM((ROWS, CTX, 2 * HEAD_WIDTH), BF16),
            pltpu.VMEM(weight.shape, BF16),
            pltpu.SemaphoreType.DMA((5,)),
            pltpu.SemaphoreType.DMA((ROWS // GROUP,)),
            pltpu.SemaphoreType.DMA,
            pltpu.SemaphoreType.DMA((2,)),
        ],
        compiler_params=pltpu.CompilerParams(vmem_limit_bytes=12 * 2**20),
        name="attend",
    )(*[pltpu.with_memory_space_constraint(x, pltpu.HBM) for x in (queries, fresh, lengths, index, table, cache, weight, up_weight)])


def down_kernel(arrived_ref, down_ref, kept_ref, near_ref, merged_ref, mask_ref):
    arrived = arrived_ref[...]
    slots = REP * CAP
    slot = iota((slots, 8 * REP), 0)
    source = (slot % 64 // 2) * 8 + slot // 64 * 2 + slot % 2
    at = iota((slots, 8 * REP), 1)
    features = dot(one_hot(at == source), arrived).astype(BF16)
    tags = dot(one_hot(at == source + 4), arrived[:, :128]).astype(BF16)
    spread = one_hot(iota((128, 256), 1) // 64 == iota((128, 256), 0))
    mask = dot(tags, spread)
    mask_ref[...] = mask.astype(BF16)
    product = dot_t(features, down_ref[...]) * mask
    product = product[:, :128] + product[:, 128:]
    product = product + pltpu.roll(product, 64, 1)
    low = iota((32, 128), 1) < 64
    parts = [
        jnp.where(low, product[64 * p:64 * p + 32], product[64 * p + 32:64 * p + 64]).astype(BF16)
        for p in range(2)
    ]
    for piece in range(TP):
        at = slice(piece * ROWS, (piece + 1) * ROWS)
        merged_ref[piece, :ROWS, :] = (
            kept_ref[at, :].astype(F32) + near_ref[at, :].astype(F32)
        ).astype(BF16)
        merged_ref[piece, ROWS:, :] = parts[piece % 2]


def down(arrived, down_weight, kept, near):
    return pl.pallas_call(
        down_kernel,
        out_shape=(
            jax.ShapeDtypeStruct((TP, 2 * ROWS, 128), BF16),
            jax.ShapeDtypeStruct((REP * CAP, 256), BF16),
        ),
        in_specs=[VMEM] * 4,
        out_specs=(VMEM,) * 2,
        compiler_params=pltpu.CompilerParams(vmem_limit_bytes=8 * 2**20),
        name="down",
    )(arrived, down_weight, kept, near)


def up_kernel(merged_ref, mask_ref, up_ref, near_ref, answer_ref, base_ref):
    mine = lax.axis_index("near")
    sums = []
    for p in range(2):
        total = merged_ref[p].astype(F32)
        for piece in range(p + 2, TP, 2):
            total = total + merged_ref[piece].astype(F32)
        base_ref[p * ROWS:(p + 1) * ROWS, :] = total[:ROWS]
        sums.append(total[ROWS:])
    shrink = (sums[0] + sums[1]).astype(BF16).astype(F32)
    turned = pltpu.roll(shrink, 64, 1)
    low = iota(shrink.shape, 1) < 64
    shrink = jnp.concatenate(
        [jnp.where(low, shrink, turned), jnp.where(low, turned, shrink)], axis=0
    ).astype(BF16)
    mask = mask_ref[pl.ds(pl.multiple_of(mine * 64, 64), 64), :]
    spread = jnp.concatenate([shrink, shrink], axis=1) * mask
    row = iota((8 * REP, 64), 0)
    at = iota((8 * REP, 64), 1)
    first = (at // 2) * 8 + (at % 2) * 2
    total = jnp.zeros((8 * REP, 128), F32)
    for half in range(2):
        near_at = TP * ROWS + half * 256
        for up_half, side in (
            (up_ref[:, half * 128:(half + 1) * 128], mine),
            (near_ref[near_at:near_at + 256, :], 1 - mine),
        ):
            answers = dot(spread, up_half).astype(BF16)
            total = total + dot(one_hot(row == first + side * 4 + half), answers)
    answer_ref[...] = total.astype(BF16)


def up(merged, mask, up_weight, near):
    return pl.pallas_call(
        up_kernel,
        out_shape=(
            jax.ShapeDtypeStruct((8 * REP, 128), BF16),
            jax.ShapeDtypeStruct((2 * ROWS, 128), F32),
        ),
        in_specs=[VMEM] * 4,
        out_specs=(VMEM,) * 2,
        compiler_params=pltpu.CompilerParams(vmem_limit_bytes=8 * 2**20),
        name="up",
    )(merged, mask, up_weight, near)


def final_kernel(returned_ref, back_ref, base_ref, residual_ref, out_ref):
    total = dot(back_ref[...], returned_ref[...]) + base_ref[...]
    total = jnp.concatenate([total[:ROWS], total[ROWS:]], axis=1)
    out_ref[...] = (residual_ref[...].astype(F32) + total).astype(BF16)


def final(returned, back, base_out, residual):
    return pl.pallas_call(
        final_kernel,
        out_shape=jax.ShapeDtypeStruct(residual.shape, BF16),
        in_specs=[VMEM] * 4,
        out_specs=VMEM,
        compiler_params=pltpu.CompilerParams(vmem_limit_bytes=8 * 2**20),
        name="final",
    )(returned, back, base_out, residual)


def exchange(x, axis):
    return lax.all_to_all(x, axis, split_axis=0, concat_axis=0, tiled=True)


def swap_near(x):
    return lax.ppermute(x, "near", [(0, 1), (1, 0)])


def on_device(
    queries,
    new_key_value,
    key_value_cache,
    lengths,
    residual,
    output_weight,
    row_adapter_index,
    adapter_storage_slot,
    adapter_down_weight,
    adapter_up_weight,
):
    up_weight = adapter_up_weight.reshape(256, 256)
    send, back, kept, pack = attend(
        queries,
        new_key_value.reshape(ROWS, 2 * HEAD_WIDTH),
        lengths.reshape(1, ROWS),
        row_adapter_index.reshape(1, ROWS),
        adapter_storage_slot.reshape(1, -1),
        key_value_cache.reshape(ROWS, CTX, 2 * HEAD_WIDTH),
        output_weight,
        up_weight,
    )
    arrived = exchange(send.reshape(REP, 8, 256), "rep").reshape(8 * REP, 256)
    near = swap_near(pack)
    down_weight = jnp.swapaxes(adapter_down_weight, 1, 2).reshape(256, 256)
    merged, mask = down(arrived, down_weight, kept, near)
    merged = exchange(merged, ("far", "near"))
    answers, base_out = up(merged, mask, up_weight, near)
    returned = exchange(answers.reshape(2 * REP, 4, 128), ("rep", "near")).reshape(8 * REP, 128)
    return final(returned, back, base_out, residual)


def solution(mesh):
    mesh = Mesh(mesh.devices.reshape(REP, TP // 2, 2), ("rep", "far", "near"))
    tp = ("far", "near")
    in_specs = (
        P("rep", tp),
        P("rep", tp, None),
        P("rep", tp, None, None),
        P("rep"),
        P("rep", tp),
        P(tp, None),
        P("rep"),
        P(),
        P("rep", tp, None),
        P("rep", None, tp),
    )
    return jax.shard_map(
        on_device, mesh=mesh, in_specs=in_specs, out_specs=P("rep", tp), check_vma=False
    )
```

```python
import functools
import math

import jax
import jax.numpy as jnp
from jax import lax
from jax.experimental import pallas as pl
from jax.experimental.pallas import tpu as pltpu
from jax.sharding import Mesh
from jax.sharding import PartitionSpec as P

HEAD_WIDTH = 128
ROWS = 32
CTX = 128
REP = 32
TP = 16
CAP = 4
GROUP = 8
F32 = jnp.float32
BF16 = jnp.bfloat16
VMEM = pl.BlockSpec(memory_space=pltpu.VMEM)
HBM = pl.BlockSpec(memory_space=pltpu.HBM)


def iota(shape, dim):
    return lax.broadcasted_iota(jnp.int32, shape, dim)


def dot(a, b):
    return jnp.dot(a, b, preferred_element_type=F32)


def dot_t(a, b):
    return lax.dot_general(a, b, (((1,), (1,)), ((), ())), preferred_element_type=F32)


def one_hot(hit):
    return jnp.where(hit, 1.0, 0.0).astype(BF16)


def to_column(row):
    size = row.shape[1]
    eye = iota((size, size), 0) == iota((size, size), 1)
    return jnp.sum(jnp.where(eye, row, 0), axis=1, keepdims=True)


def to_row(column):
    size = column.shape[0]
    eye = iota((size, size), 0) == iota((size, size), 1)
    return jnp.sum(jnp.where(eye, column, 0), axis=0, keepdims=True)


def attend_kernel(
    q_hbm, fresh_hbm, lengths_hbm, index_hbm, table_hbm, kv_hbm, weight_hbm, up_hbm,
    send_ref, back_ref, kept_ref, pack_ref,
    attended_ref, q_ref, fresh_ref, lengths_ref, index_ref, table_ref, kv_ref, weight_ref, small_sems, sems, weight_sem, up_sems,
):
    groups = ROWS // GROUP
    small = [
        pltpu.make_async_copy(src, dst, small_sems.at[i])
        for i, (src, dst) in enumerate((
            (index_hbm, index_ref),
            (table_hbm, table_ref),
            (lengths_hbm, lengths_ref),
            (q_hbm, q_ref),
            (fresh_hbm, fresh_ref),
        ))
    ]
    for copy in small:
        copy.start()
    copies = [
        pltpu.make_async_copy(
            kv_hbm.at[pl.ds(g % 2 * 16, 16), :, pl.ds(g // 2 * HEAD_WIDTH, HEAD_WIDTH)],
            kv_ref.at[pl.ds(g % 2 * 16, 16), :, pl.ds(g // 2 * HEAD_WIDTH, HEAD_WIDTH)],
            sems.at[g],
        )
        for g in range(4)
    ]
    for copy in copies:
        copy.start()
    weight_copy = pltpu.make_async_copy(weight_hbm, weight_ref, weight_sem)
    weight_copy.start()
    half_rows = TP * ROWS
    up_copies = [
        pltpu.make_async_copy(
            up_hbm.at[:, pl.ds(half * 128, 128)],
            pack_ref.at[pl.ds(half_rows + half * 256, 256)],
            up_sems.at[half],
        )
        for half in range(2)
    ]
    for copy in up_copies:
        copy.start()
    for copy in small:
        copy.wait()

    table = table_ref[...]
    index = to_column(index_ref[...])
    size = table.shape[1]
    slot = jnp.sum(jnp.where(index == iota((ROWS, size), 1), table, 0), axis=1, keepdims=True)
    owner = slot // 4
    local = slot - owner * 4
    owner_row = to_row(owner)
    earlier = (owner == owner_row) & (iota((ROWS, ROWS), 0) > iota((ROWS, ROWS), 1))
    rank = jnp.sum(jnp.where(earlier, 1, 0), axis=1, keepdims=True)
    target = owner * CAP + rank
    back = iota((ROWS, 2 * REP * CAP), 1)
    for half in range(2):
        back_ref[half * ROWS:(half + 1) * ROWS, :] = one_hot(back == target * 2 + half)
    place = to_row(owner * 8 + rank)
    tags = one_hot(iota((ROWS, 2 * HEAD_WIDTH), 1) == local)
    rows_out = iota((8 * REP, ROWS), 0)
    place_tag = one_hot(rows_out == place + 4)
    place_row = one_hot(rows_out == place)

    lengths = to_column(lengths_ref[...])
    for copy in copies[:2]:
        copy.wait()
    scale = 1.0 / math.sqrt(HEAD_WIDTH)
    q = q_ref[...].astype(F32)
    heads = jnp.concatenate([q[:, :HEAD_WIDTH], q[:, HEAD_WIDTH:]], axis=0)
    fresh = fresh_ref[...].astype(F32)
    fresh_key = jnp.concatenate([fresh[:, :HEAD_WIDTH]] * 2, axis=0)
    own = jnp.sum(heads * fresh_key, axis=1, keepdims=True) * scale
    empty = jnp.zeros_like(heads)
    heads = jnp.concatenate(
        [jnp.concatenate([heads, empty], axis=1), jnp.concatenate([empty, heads], axis=1)], axis=0
    ).astype(BF16)
    column = iota((CTX, 4 * ROWS), 1)
    column = column % ROWS - column // (2 * ROWS) * (ROWS // 2)
    turned = jnp.zeros((CTX, 4 * ROWS), F32)
    for r in range(ROWS // 2):
        keys = jnp.concatenate(
            [kv_ref[r, :, :HEAD_WIDTH], kv_ref[r + ROWS // 2, :, :HEAD_WIDTH]], axis=1
        )
        turned = jnp.where(column == r, dot_t(keys, heads), turned)
    turned = turned.T
    early = iota((2 * ROWS, CTX), 0) % ROWS < ROWS // 2
    turned = jnp.where(early, turned[:2 * ROWS], turned[2 * ROWS:])
    live = iota((2 * ROWS, CTX), 1) < jnp.concatenate([lengths] * 2, axis=0)
    scores = jnp.where(live, turned * scale, -1e30)
    top = jnp.maximum(jnp.max(scores, axis=1, keepdims=True), own)
    weights = jnp.where(live, jnp.exp(scores - top), 0.0)
    own_weight = jnp.exp(own - top)
    denom = jnp.sum(weights, axis=1, keepdims=True) + own_weight
    probs = weights / denom
    own_prob = (own_weight / denom).astype(BF16).astype(F32)
    for copy in copies[2:]:
        copy.wait()
    row_at = iota((2 * GROUP, CTX), 0) % GROUP
    for g in range(groups):
        at = slice(g * GROUP, (g + 1) * GROUP)
        both = slice(ROWS + g * GROUP, ROWS + (g + 1) * GROUP)
        part_probs = jnp.concatenate([probs[at], probs[both]], axis=0)
        spread = jnp.concatenate(
            [jnp.where(row_at == i, part_probs, 0.0) for i in range(GROUP)], axis=1
        ).astype(BF16)
        values = kv_ref[g * GROUP:(g + 1) * GROUP, :, HEAD_WIDTH:].reshape(GROUP * CTX, HEAD_WIDTH)
        mixed = dot(spread, values)
        value = fresh[at, HEAD_WIDTH:]
        attended_ref[at, :] = jnp.concatenate(
            [mixed[:GROUP] + own_prob[at] * value, mixed[GROUP:] + own_prob[both] * value], axis=1
        )
    attended = attended_ref[...].astype(BF16)
    weight_copy.wait()
    mine = lax.axis_index("near")
    for piece in range(TP):
        for ref, half in ((pack_ref, 1 - mine), (kept_ref, mine)):
            at = pl.multiple_of((2 * piece + half) * 128, 128)
            ref[piece * ROWS:(piece + 1) * ROWS, :] = dot(
                attended, weight_ref[:, pl.ds(at, 128)]
            ).astype(BF16)
    send_ref[...] = (dot(place_row, attended) + dot(place_tag, tags)).astype(BF16)
    for copy in up_copies:
        copy.wait()


def attend(queries, fresh, lengths, index, table, cache, weight, up_weight):
    return pl.pallas_call(
        attend_kernel,
        out_shape=(
            jax.ShapeDtypeStruct((8 * REP, 2 * HEAD_WIDTH), BF16),
            jax.ShapeDtypeStruct((2 * ROWS, 2 * REP * CAP), BF16),
            jax.ShapeDtypeStruct((TP * ROWS, 128), BF16),
            jax.ShapeDtypeStruct((TP * ROWS + 512, 128), BF16),
        ),
        in_specs=[HBM] * 8,
        out_specs=(VMEM,) * 4,
        scratch_shapes=[
            pltpu.VMEM(queries.shape, F32),
            pltpu.VMEM(queries.shape, BF16),
            pltpu.VMEM(fresh.shape, BF16),
            pltpu.VMEM(lengths.shape, jnp.int32),
            pltpu.VMEM(index.shape, jnp.int32),
            pltpu.VMEM(table.shape, jnp.int32),
            pltpu.VMEM((ROWS, CTX, 2 * HEAD_WIDTH), BF16),
            pltpu.VMEM(weight.shape, BF16),
            pltpu.SemaphoreType.DMA((5,)),
            pltpu.SemaphoreType.DMA((4,)),
            pltpu.SemaphoreType.DMA,
            pltpu.SemaphoreType.DMA((2,)),
        ],
        compiler_params=pltpu.CompilerParams(vmem_limit_bytes=12 * 2**20),
        name="attend",
    )(*[pltpu.with_memory_space_constraint(x, pltpu.HBM) for x in (queries, fresh, lengths, index, table, cache, weight, up_weight)])


def down_kernel(arrived_ref, down_ref, kept_ref, near_ref, merged_ref, mask_ref):
    arrived = arrived_ref[...]
    slots = REP * CAP
    slot = iota((slots, 8 * REP), 0)
    source = (slot % 64 // 2) * 8 + slot // 64 * 2 + slot % 2
    at = iota((slots, 8 * REP), 1)
    features = dot(one_hot(at == source), arrived).astype(BF16)
    tags = dot(one_hot(at == source + 4), arrived[:, :128]).astype(BF16)
    spread = one_hot(iota((128, 256), 1) // 64 == iota((128, 256), 0))
    mask = dot(tags, spread)
    mask_ref[...] = mask.astype(BF16)
    product = dot_t(features, down_ref[...]) * mask
    product = product[:, :128] + product[:, 128:]
    product = product + pltpu.roll(product, 64, 1)
    low = iota((32, 128), 1) < 64
    parts = [
        jnp.where(low, product[64 * p:64 * p + 32], product[64 * p + 32:64 * p + 64]).astype(BF16)
        for p in range(2)
    ]
    for piece in range(TP):
        at = slice(piece * ROWS, (piece + 1) * ROWS)
        merged_ref[piece, :ROWS, :] = (
            kept_ref[at, :].astype(F32) + near_ref[at, :].astype(F32)
        ).astype(BF16)
        merged_ref[piece, ROWS:, :] = parts[piece % 2]


def down(arrived, down_weight, kept, near):
    return pl.pallas_call(
        down_kernel,
        out_shape=(
            jax.ShapeDtypeStruct((TP, 2 * ROWS, 128), BF16),
            jax.ShapeDtypeStruct((REP * CAP, 256), BF16),
        ),
        in_specs=[VMEM] * 4,
        out_specs=(VMEM,) * 2,
        compiler_params=pltpu.CompilerParams(vmem_limit_bytes=8 * 2**20),
        name="down",
    )(arrived, down_weight, kept, near)


def up_kernel(merged_ref, mask_ref, up_ref, near_ref, answer_ref, base_ref):
    mine = lax.axis_index("near")
    sums = []
    for p in range(2):
        total = merged_ref[p].astype(F32)
        for piece in range(p + 2, TP, 2):
            total = total + merged_ref[piece].astype(F32)
        base_ref[p * ROWS:(p + 1) * ROWS, :] = total[:ROWS]
        sums.append(total[ROWS:])
    shrink = (sums[0] + sums[1]).astype(BF16).astype(F32)
    turned = pltpu.roll(shrink, 64, 1)
    low = iota(shrink.shape, 1) < 64
    shrink = jnp.concatenate(
        [jnp.where(low, shrink, turned), jnp.where(low, turned, shrink)], axis=0
    ).astype(BF16)
    mask = mask_ref[pl.ds(pl.multiple_of(mine * 64, 64), 64), :]
    spread = jnp.concatenate([shrink, shrink], axis=1) * mask
    row = iota((8 * REP, 64), 0)
    at = iota((8 * REP, 64), 1)
    first = (at // 2) * 8 + (at % 2) * 2
    total = jnp.zeros((8 * REP, 128), F32)
    for half in range(2):
        near_at = TP * ROWS + half * 256
        for up_half, side in (
            (up_ref[:, half * 128:(half + 1) * 128], mine),
            (near_ref[near_at:near_at + 256, :], 1 - mine),
        ):
            answers = dot(spread, up_half).astype(BF16)
            total = total + dot(one_hot(row == first + side * 4 + half), answers)
    answer_ref[...] = total.astype(BF16)


def up(merged, mask, up_weight, near):
    return pl.pallas_call(
        up_kernel,
        out_shape=(
            jax.ShapeDtypeStruct((8 * REP, 128), BF16),
            jax.ShapeDtypeStruct((2 * ROWS, 128), F32),
        ),
        in_specs=[VMEM] * 4,
        out_specs=(VMEM,) * 2,
        compiler_params=pltpu.CompilerParams(vmem_limit_bytes=8 * 2**20),
        name="up",
    )(merged, mask, up_weight, near)


def final_kernel(returned_ref, back_ref, base_ref, residual_ref, out_ref):
    total = dot(back_ref[...], returned_ref[...]) + base_ref[...]
    total = jnp.concatenate([total[:ROWS], total[ROWS:]], axis=1)
    out_ref[...] = (residual_ref[...].astype(F32) + total).astype(BF16)


def final(returned, back, base_out, residual):
    return pl.pallas_call(
        final_kernel,
        out_shape=jax.ShapeDtypeStruct(residual.shape, BF16),
        in_specs=[VMEM] * 4,
        out_specs=VMEM,
        compiler_params=pltpu.CompilerParams(vmem_limit_bytes=8 * 2**20),
        name="final",
    )(returned, back, base_out, residual)


def exchange(x, axis):
    return lax.all_to_all(x, axis, split_axis=0, concat_axis=0, tiled=True)


def swap_near(x):
    return lax.ppermute(x, "near", [(0, 1), (1, 0)])


def on_device(
    queries,
    new_key_value,
    key_value_cache,
    lengths,
    residual,
    output_weight,
    row_adapter_index,
    adapter_storage_slot,
    adapter_down_weight,
    adapter_up_weight,
):
    up_weight = adapter_up_weight.reshape(256, 256)
    send, back, kept, pack = attend(
        queries,
        new_key_value.reshape(ROWS, 2 * HEAD_WIDTH),
        lengths.reshape(1, ROWS),
        row_adapter_index.reshape(1, ROWS),
        adapter_storage_slot.reshape(1, -1),
        key_value_cache.reshape(ROWS, CTX, 2 * HEAD_WIDTH),
        output_weight,
        up_weight,
    )
    arrived = exchange(send.reshape(REP, 8, 256), "rep").reshape(8 * REP, 256)
    near = swap_near(pack)
    down_weight = jnp.swapaxes(adapter_down_weight, 1, 2).reshape(256, 256)
    merged, mask = down(arrived, down_weight, kept, near)
    merged = exchange(merged, ("far", "near"))
    answers, base_out = up(merged, mask, up_weight, near)
    returned = exchange(answers.reshape(2 * REP, 4, 128), ("rep", "near")).reshape(8 * REP, 128)
    return final(returned, back, base_out, residual)


def solution(mesh):
    mesh = Mesh(mesh.devices.reshape(REP, TP // 2, 2), ("rep", "far", "near"))
    tp = ("far", "near")
    in_specs = (
        P("rep", tp),
        P("rep", tp, None),
        P("rep", tp, None, None),
        P("rep"),
        P("rep", tp),
        P(tp, None),
        P("rep"),
        P(),
        P("rep", tp, None),
        P("rep", None, tp),
    )
    return jax.shard_map(
        on_device, mesh=mesh, in_specs=in_specs, out_specs=P("rep", tp), check_vma=False
    )
```
